32 devices in a mesh: fsdp: 8 (over y, x, core), tensor: 4 (over z).
Axes of the slice: x: 2, y: 2, z: 4, core: 2. Of those that a mesh axis runs over, the one named last changes fastest.
Arguments:
- inputs: bfloat16 [8192, 1024], P(('fsdp', 'tensor')), may hold values from -6 to 6
- qkv_weight: bfloat16 [1024, 3, 1024], P('fsdp', None, 'tensor'), may hold values from -0.1875 to 0.1875
- qv_bias: bfloat16 [2, 1024], P(None, 'tensor'), may hold values from -3 to 3
- out_weight: bfloat16 [1024, 1024], P('tensor', 'fsdp'), may hold values from -0.5 to 0.5
- out_bias: bfloat16 [1024], replicated, may hold values from -3 to 3
- up_weight: bfloat16 [1024, 4096], P('fsdp', 'tensor'), may hold values from -0.1875 to 0.1875
- up_bias: bfloat16 [4096], P('tensor'), may hold values from -3 to 3
- down_weight: bfloat16 [4096, 1024], P('tensor', 'fsdp'), may hold values from -0.1875 to 0.1875
- down_bias: bfloat16 [1024], replicated, may hold values from -3 to 3
- norm1_gain: bfloat16 [1024], replicated, may hold values from 0.25 to 1.75
- norm1_shift: bfloat16 [1024], replicated, may hold values from -2 to 2
- norm2_gain: bfloat16 [1024], replicated, may hold values from 0.25 to 1.75
- norm2_shift: bfloat16 [1024], replicated, may hold values from -2 to 2
- cotangent: bfloat16 [8192, 1024], P(('fsdp', 'tensor')), may hold values from -6 to 6
Outputs:
- block_out: bfloat16 [8192, 1024], P(('fsdp', 'tensor'))
- input_grad: float32 [8192, 1024], P(('fsdp', 'tensor'))
- qkv_weight_grad: float32 [1024, 3, 1024], P('fsdp', None, 'tensor')
- qv_bias_grad: float32 [2, 1024], P(None, 'tensor')
- out_weight_grad: float32 [1024, 1024], P('tensor', 'fsdp')
- out_bias_grad: float32 [1024], replicated
- up_weight_grad: float32 [1024, 4096], P('fsdp', 'tensor')
- up_bias_grad: float32 [4096], P('tensor')
- down_weight_grad: float32 [4096, 1024], P('tensor', 'fsdp')
- down_bias_grad: float32 [1024], replicated
- norm1_gain_grad: float32 [1024], replicated
- norm1_shift_grad: float32 [1024], replicated
- norm2_gain_grad: float32 [1024], replicated
- norm2_shift_grad: float32 [1024], replicated
The draws below stay inside these ranges and needn't reach their ends.
All inputs are finite; a program needn't handle non-finite values.
Results may differ from the reference program's by a relative error of at most 0.02.
Values may be sent and summed in bfloat16 or wider, within the bound.
A program may use at most 128 MiB of HBM per device.

```python
import jax
import jax.numpy as jnp
from jax import lax

D = 1024
HEADS = 16
HEAD_DIM = 64
FF = 4096
LEN = 1024
TOKENS = 8192
N_TENSOR = 4


def block_scale(key, dims, split, smallest, top_value):
    gain = 1.0
    for position, shards_of in split:
        heights = jax.random.uniform(jax.random.fold_in(jax.random.fold_in(key, 6), position), (shards_of,), jnp.float32, smallest / len(split), top_value / len(split))
        gain = gain * jnp.repeat(jnp.exp(heights), dims[position] // shards_of).reshape((-1,) + (1,) * (len(dims) - 1 - position))
    return gain


def noise(own_key, extent, scale, most, shards=(), held_as=jnp.bfloat16):
    result = jax.random.normal(own_key, extent, jnp.float32) * scale
    if len(shards) > 0:
        result = block_scale(own_key, extent, shards, -0.22, 0.18) * result
    return jnp.clip(result, min=-most, max=most).astype(held_as)


def setup_inputs(seed: int = 0) -> dict:
    keys = jax.random.split(jax.random.key(seed), 15)
    inputs = noise(keys[0], (TOKENS, D), 1.0, 6.0, ((0, 32),))
    qkv_weight = noise(keys[1], (D, 3, D), D ** -0.5, 0.1875, ((0, 8), (2, 4)))
    qv_bias = noise(keys[2], (2, D), 0.5, 3.0, ((1, 4),))
    out_weight = noise(keys[3], (D, D), (D // 8) ** -0.5, 0.5, ((0, 4), (1, 8)))
    out_bias = noise(keys[4], (D,), 0.5, 3.0)
    up_weight = noise(keys[5], (D, FF), D ** -0.5, 0.1875, ((0, 8), (1, 4)))
    up_bias = noise(keys[6], (FF,), 0.5, 3.0, ((0, 4),))
    down_weight = noise(keys[7], (FF, D), (FF // 4) ** -0.5, 0.1875, ((0, 4), (1, 8)))
    down_bias = noise(keys[8], (D,), 0.5, 3.0)
    norm1_gain = jnp.clip(1.0 + 0.15 * jax.random.normal(keys[9], (D,), jnp.float32), 0.25, 1.75).astype(jnp.bfloat16)
    norm1_shift = noise(keys[10], (D,), 0.3, 2.0)
    norm2_gain = jnp.clip(1.0 + 0.15 * jax.random.normal(keys[11], (D,), jnp.float32), 0.25, 1.75).astype(jnp.bfloat16)
    norm2_shift = noise(keys[12], (D,), 0.3, 2.0)
    cotangent = noise(keys[13], (TOKENS, D), 1.0, 6.0, ((0, 32),))
    return dict(inputs=inputs, qkv_weight=qkv_weight, qv_bias=qv_bias, out_weight=out_weight, out_bias=out_bias, up_weight=up_weight, up_bias=up_bias, down_weight=down_weight, down_bias=down_bias, norm1_gain=norm1_gain, norm1_shift=norm1_shift, norm2_gain=norm2_gain, norm2_shift=norm2_shift, cotangent=cotangent)


@jax.custom_vjp
def low(v):
    return lax.optimization_barrier(v.astype(jnp.bfloat16)).astype(jnp.float32)

@jax.custom_vjp
def low_back(v):
    return v

def low_keep(v):
    return (low(v), None)

def low_pass(kept, grad):
    return (grad,)

def back_keep(v):
    return (v, None)

def back_low(kept, grad):
    return (low(grad),)
low.defvjp(low_keep, low_pass)
low_back.defvjp(back_keep, back_low)
layer_eps = 1e-05
highest = lax.Precision.HIGHEST

def layer_norm(rows, norm_gain, norm_shift):
    average = lax.optimization_barrier(jnp.mean(rows, axis=1, keepdims=True))
    centred = rows - average
    spread = lax.optimization_barrier(jnp.mean(centred * centred, axis=1, keepdims=True))
    return centred * lax.rsqrt(spread + layer_eps) * norm_gain + norm_shift

def attend_sequence(pieces):
    queries, key_rows, value_rows = pieces
    raw_scores = jnp.einsum('qhd,khd->hqk', queries, key_rows, precision=highest)
    places = jnp.arange(LEN).astype(jnp.float32)
    offsets = places[None, :] - places[:, None]
    slopes = jnp.exp2(-8.0 * (jnp.arange(HEADS).astype(jnp.float32) + 1.0) / HEADS)
    scores = low_back(raw_scores) * HEAD_DIM ** (-0.5) + slopes[:, None, None] * offsets[None]
    scores = jnp.where(offsets[None] <= 0.0, scores, -1e+30)
    probability = jax.nn.softmax(scores, axis=-1)
    return jnp.einsum('hqk,khd->qhd', low(probability), value_rows, precision=highest)

def by_heads(rows):
    return rows.reshape(TOKENS // LEN, LEN, HEADS, HEAD_DIM)

def forward(inputs, qkv_weight, qv_bias, out_weight, out_bias, up_weight, up_bias, down_weight, down_bias, norm1_gain, norm1_shift, norm2_gain, norm2_shift):
    group_width = D // N_TENSOR
    hidden_width = FF // N_TENSOR
    attn_in = low(layer_norm(inputs, norm1_gain, norm1_shift))
    projected = jnp.concatenate([jnp.einsum('td,dcf->tcf', low_back(attn_in), qkv_weight[:, :, group * group_width:(group + 1) * group_width], precision=highest) for group in range(N_TENSOR)], axis=2)
    queries = low(low_back(projected[:, 0] + qv_bias[0]))
    keys_all = low(low_back(projected[:, 1]))
    values_all = low(low_back(projected[:, 2] + qv_bias[1]))
    attended = lax.map(jax.checkpoint(attend_sequence), (by_heads(queries), by_heads(keys_all), by_heads(values_all)))
    mixed = low(low_back(attended.reshape(TOKENS, D)))
    attn_sum = jnp.zeros((TOKENS, D), jnp.float32)
    for group in range(N_TENSOR):
        part_rows = slice(group * group_width, (group + 1) * group_width)
        attn_sum = attn_sum + low(jnp.dot(mixed[:, part_rows], out_weight[part_rows], precision=highest))
    hidden1 = inputs + low_back(attn_sum) + out_bias
    mlp_in = low(layer_norm(hidden1, norm2_gain, norm2_shift))
    raised = jnp.concatenate([jnp.dot(low_back(mlp_in), up_weight[:, group * hidden_width:(group + 1) * hidden_width], precision=highest) for group in range(N_TENSOR)], axis=1)
    raised = low_back(raised + up_bias)
    activated = low(jax.nn.gelu(raised, approximate=True))
    mlp_sum = jnp.zeros((TOKENS, D), jnp.float32)
    for group in range(N_TENSOR):
        part_rows = slice(group * hidden_width, (group + 1) * hidden_width)
        mlp_sum = mlp_sum + low(jnp.dot(activated[:, part_rows], down_weight[part_rows], precision=highest))
    return hidden1 + low_back(mlp_sum) + down_bias

def reference(inputs, qkv_weight, qv_bias, out_weight, out_bias, up_weight, up_bias, down_weight, down_bias, norm1_gain, norm1_shift, norm2_gain, norm2_shift, cotangent):
    params = tuple((item.astype(jnp.float32) for item in (inputs, qkv_weight, qv_bias, out_weight, out_bias, up_weight, up_bias, down_weight, down_bias, norm1_gain, norm1_shift, norm2_gain, norm2_shift)))
    block_out, pullback = jax.vjp(forward, *params)
    grads = pullback(cotangent.astype(jnp.float32))
    return (block_out.astype(jnp.bfloat16), grads[0], grads[1], grads[2], grads[3], grads[4], grads[5], grads[6], grads[7], grads[8], grads[9], grads[10], grads[11], grads[12])
```

```python
from functools import partial

import jax
import jax.numpy as jnp
from jax import lax
from jax.experimental import pallas as pl
from jax.experimental.pallas import tpu as pltpu
from jax.sharding import Mesh, PartitionSpec as P

D = 1024
HEADS = 16
HEAD_DIM = 64
FF = 4096
SEQ_LEN = 1024


layer_eps = 1e-05


def normalize(rows, norm_gain, norm_shift):
    average = jnp.mean(rows, axis=1, keepdims=True)
    centred = rows - average
    spread = jnp.mean(centred * centred, axis=1, keepdims=True)
    inverse = lax.rsqrt(spread + layer_eps)
    scaled = centred * inverse
    return (scaled * norm_gain + norm_shift, scaled, inverse)


def normalize_back(upper, scaled, inverse, norm_gain):
    gain_grad = jnp.sum(upper * scaled, axis=0)
    shift_grad = jnp.sum(upper, axis=0)
    inner = upper * norm_gain
    lower = inverse * (
        inner
        - jnp.mean(inner, axis=1, keepdims=True)
        - scaled * jnp.mean(inner * scaled, axis=1, keepdims=True)
    )
    return (lower, gain_grad, shift_grad)


def head_mask(shape, head):
    lanes = lax.broadcasted_iota(jnp.int32, shape, 1)
    return (lanes >= head * HEAD_DIM) & (lanes < (head + 1) * HEAD_DIM)


def rows_dot(left, right):
    return lax.dot_general(
        left, right, (((1,), (1,)), ((), ())), preferred_element_type=jnp.float32
    )


def cols_dot(left, right):
    return lax.dot_general(
        left, right, (((0,), (0,)), ((), ())), preferred_element_type=jnp.float32
    )


def block_scores(query_block, keys_seen, slope, start, finish):
    raw = rows_dot(query_block, keys_seen) * HEAD_DIM ** (-0.5)
    shape = raw.shape
    offsets = lax.broadcasted_iota(jnp.int32, shape, 1) - (
        lax.broadcasted_iota(jnp.int32, shape, 0) + start
    )
    scores = raw + slope * offsets.astype(jnp.float32)
    return jnp.where(offsets <= 0, scores, -1e30)


def forward_kernel(heads, block_rows, slopes_ref, q_ref, k_ref, v_ref, mixed_ref, lse_ref):
    length, width = q_ref.shape
    for start in range(0, length, block_rows):
        finish = start + block_rows
        query_block = q_ref[start:finish]
        keys_seen = k_ref[:finish]
        values_seen = v_ref[:finish]
        out = jnp.zeros((block_rows, width), jnp.float32)
        lse = jnp.zeros((block_rows, 128), jnp.float32)
        lanes = lax.broadcasted_iota(jnp.int32, lse.shape, 1)
        zero = jnp.zeros_like(query_block)
        for head in range(heads):
            mask = head_mask(query_block.shape, head)
            scores = block_scores(
                jnp.where(mask, query_block, zero), keys_seen, slopes_ref[head], start, finish
            )
            top = jnp.max(scores, axis=1, keepdims=True)
            terms = jnp.exp(scores - top)
            total = jnp.sum(terms, axis=1, keepdims=True)
            probability = (terms * (1.0 / total)).astype(jnp.bfloat16)
            part = jnp.dot(probability, values_seen, preferred_element_type=jnp.float32)
            out = jnp.where(head_mask(out.shape, head), part, out)
            lse = jnp.where(lanes == head, top + jnp.log(total), lse)
        mixed_ref[start:finish] = out.astype(jnp.bfloat16)
        lse_ref[start:finish] = lse


def backward_kernel(
    heads,
    block_rows,
    slopes_ref,
    q_ref,
    k_ref,
    v_ref,
    grad_ref,
    lse_ref,
    dq_ref,
    dk_ref,
    dv_ref,
    bias_ref,
    dk_total,
    dv_total,
):
    length, width = q_ref.shape
    dk_total[...] = jnp.zeros_like(dk_total)
    dv_total[...] = jnp.zeros_like(dv_total)
    dq_sum = jnp.zeros((1, width), jnp.float32)
    for start in range(0, length, block_rows):
        finish = start + block_rows
        query_block = q_ref[start:finish]
        grad_block = grad_ref[start:finish]
        keys_seen = k_ref[:finish]
        values_seen = v_ref[:finish]
        zero = jnp.zeros_like(query_block)
        dq = jnp.zeros((block_rows, width), jnp.float32)
        for head in range(heads):
            mask = head_mask(query_block.shape, head)
            query_head = jnp.where(mask, query_block, zero)
            grad_head = jnp.where(mask, grad_block, zero)
            scores = block_scores(query_head, keys_seen, slopes_ref[head], start, finish)
            probability = jnp.exp(scores - lse_ref[start:finish, head : head + 1])
            prob_grad = rows_dot(grad_head, values_seen)
            centre = jnp.sum(probability * prob_grad, axis=1, keepdims=True)
            score_grad = (probability * (prob_grad - centre) * HEAD_DIM ** (-0.5)).astype(
                jnp.bfloat16
            )
            part = jnp.dot(score_grad, keys_seen, preferred_element_type=jnp.float32)
            dq = jnp.where(head_mask(dq.shape, head), part, dq)
            dk_total[:finish] += cols_dot(score_grad, query_head)
            dv_total[:finish] += cols_dot(probability.astype(jnp.bfloat16), grad_head)
        dq_low = dq.astype(jnp.bfloat16)
        dq_ref[start:finish] = dq_low
        dq_sum += jnp.sum(dq_low.astype(jnp.float32), axis=0, keepdims=True)
    dk_ref[...] = dk_total[...].astype(jnp.bfloat16)
    dv_low = dv_total[...].astype(jnp.bfloat16)
    dv_ref[...] = dv_low
    dv_sum = jnp.sum(dv_low.astype(jnp.float32), axis=0, keepdims=True)
    bias_ref[0, 0:1] = dq_sum
    bias_ref[0, 1:2] = dv_sum


def attention_forward(queries, keys_all, values_all, slopes, heads, seq_length):
    rows, width = queries.shape
    block = pl.BlockSpec((seq_length, width), lambda s: (s, 0))
    return pl.pallas_call(
        partial(forward_kernel, heads, min(256, seq_length)),
        grid=(rows // seq_length,),
        in_specs=[pl.BlockSpec(memory_space=pltpu.SMEM), block, block, block],
        out_specs=[block, pl.BlockSpec((seq_length, 128), lambda s: (s, 0))],
        out_shape=[
            jax.ShapeDtypeStruct((rows, width), jnp.bfloat16),
            jax.ShapeDtypeStruct((rows, 128), jnp.float32),
        ],
        compiler_params=pltpu.CompilerParams(vmem_limit_bytes=40 * 2**20),
        cost_estimate=pl.CostEstimate(
            flops=4 * heads * rows * seq_length * HEAD_DIM,
            bytes_accessed=10 * rows * width,
            transcendentals=heads * rows * seq_length // 2,
        ),
        name="attention_forward",
    )(slopes, queries, keys_all, values_all)


def attention_backward(queries, keys_all, values_all, mixed_grad, lse, slopes, heads, seq_length):
    rows, width = queries.shape
    seqs = rows // seq_length
    block = pl.BlockSpec((seq_length, width), lambda s: (s, 0))
    low = jax.ShapeDtypeStruct((rows, width), jnp.bfloat16)
    return pl.pallas_call(
        partial(backward_kernel, heads, min(256, seq_length)),
        grid=(seqs,),
        in_specs=[pl.BlockSpec(memory_space=pltpu.SMEM)]
        + [block] * 4
        + [pl.BlockSpec((seq_length, 128), lambda s: (s, 0))],
        out_specs=[block, block, block, pl.BlockSpec((1, 2, width), lambda s: (s, 0, 0))],
        out_shape=[low, low, low, jax.ShapeDtypeStruct((seqs, 2, width), jnp.float32)],
        scratch_shapes=[pltpu.VMEM((seq_length, width), jnp.float32)] * 2,
        compiler_params=pltpu.CompilerParams(vmem_limit_bytes=40 * 2**20),
        cost_estimate=pl.CostEstimate(
            flops=10 * heads * rows * seq_length * HEAD_DIM,
            bytes_accessed=14 * rows * width,
            transcendentals=heads * rows * seq_length // 2,
        ),
        name="attention_backward",
    )(slopes, queries, keys_all, values_all, mixed_grad, lse)


def swap_places(array):
    lines, side = lax.axis_size("y"), lax.axis_size("a")
    pairs = [
        ((y * side + a) * side + z, (y * side + z) * side + a)
        for y in range(lines)
        for a in range(side)
        for z in range(side)
    ]
    return lax.ppermute(array, ("y", "a", "z"), pairs)


def exchange(array, axis, mask):
    size = lax.axis_size(axis)
    return lax.ppermute(array, axis, [(i, i ^ mask) for i in range(size)])


def masks_of(size):
    return [1 << bit for bit in reversed(range(size.bit_length() - 1))]


def gather_rows(block, axis):
    size = lax.axis_size(axis)
    index = lax.axis_index(axis)
    held = block
    for place, mask in enumerate(masks_of(size)):
        other = exchange(held, axis, mask)
        upper = (index & mask) != 0
        held = jnp.stack(
            [jnp.where(upper, other, held), jnp.where(upper, held, other)], axis=place
        )
    return held.reshape((size * block.shape[0],) + block.shape[1:])


def scatter_rows(array, axis):
    size = lax.axis_size(axis)
    index = lax.axis_index(axis)
    masks = masks_of(size)
    held = array.reshape((2,) * len(masks) + (array.shape[0] // size,) + array.shape[1:])
    for place, mask in reversed(list(enumerate(masks))):
        upper = (index & mask) != 0
        first = lax.index_in_dim(held, 0, place, keepdims=False)
        second = lax.index_in_dim(held, 1, place, keepdims=False)
        sent = jnp.where(upper, first, second).astype(jnp.bfloat16)
        kept = jnp.where(upper, second, first).astype(jnp.float32)
        held = kept + exchange(sent, axis, mask).astype(jnp.float32)
    return held.astype(jnp.float32)


def sum_everywhere(array):
    axes = ("y", "a", "z")
    size = lax.axis_size("y") * lax.axis_size("a") * lax.axis_size("z")
    for mask in reversed(masks_of(size)):
        array = array + lax.ppermute(array, axes, [(i, i ^ mask) for i in range(size)])
    return array


def whole_weight(shard):
    return gather_rows(lax.all_gather(swap_places(shard), "z", axis=0, tiled=True), "y")


def owned_grad(grad):
    half = scatter_rows(grad.astype(jnp.bfloat16), "y").astype(jnp.bfloat16)
    part = lax.psum_scatter(half, "z", scatter_dimension=0, tiled=True)
    return swap_places(part).astype(jnp.float32)


def body(
    inputs,
    qkv_weight,
    qv_bias,
    out_weight,
    out_bias,
    up_weight,
    up_bias,
    down_weight,
    down_bias,
    norm1_gain,
    norm1_shift,
    norm2_gain,
    norm2_shift,
    cotangent,
):
    floats = jnp.float32
    halves = jnp.bfloat16
    role = lax.axis_index("a")
    owner = lax.axis_index("z")
    shard_rows = qkv_weight.shape[0]
    width = qkv_weight.shape[2]
    hidden = up_weight.shape[1]
    heads = width // HEAD_DIM

    here = swap_places(inputs)
    qkv_whole = whole_weight(qkv_weight.reshape(shard_rows, 3 * width))
    out_whole = whole_weight(out_weight.T)
    up_whole = whole_weight(up_weight)
    down_whole = whole_weight(down_weight.T)
    biases = swap_places(jnp.concatenate([qv_bias.reshape(-1), up_bias]))
    qv_here = biases[: 2 * width].reshape(2, width).astype(floats)
    up_bias_here = biases[2 * width :].astype(floats)
    upstream_low = swap_places(cotangent)
    upstream = upstream_low.astype(floats)

    input_float = here.astype(floats)
    gain_first = norm1_gain.astype(floats)
    gain_second = norm2_gain.astype(floats)
    normed1, scaled1, inverse1 = normalize(input_float, gain_first, norm1_shift.astype(floats))
    attn_rows = gather_rows(normed1.astype(halves), "a")
    seq_length = min(SEQ_LEN, attn_rows.shape[0])
    head_index = role * heads + jnp.arange(heads)
    slopes = jnp.exp2(-8.0 * (head_index.astype(floats) + 1.0) / HEADS)

    projected = jnp.dot(attn_rows, qkv_whole, preferred_element_type=floats)
    queries = (projected[:, :width] + qv_here[0]).astype(halves)
    keys_all = projected[:, width : 2 * width].astype(halves)
    values_all = (projected[:, 2 * width :] + qv_here[1]).astype(halves)
    mixed, lse = attention_forward(queries, keys_all, values_all, slopes, heads, seq_length)
    attn_sum = scatter_rows(
        jnp.einsum("tf,df->td", mixed, out_whole, preferred_element_type=floats).astype(halves),
        "a",
    )
    hidden1 = input_float + attn_sum + out_bias.astype(floats)
    normed2, scaled2, inverse2 = normalize(hidden1, gain_second, norm2_shift.astype(floats))
    mlp_rows = gather_rows(normed2.astype(halves), "a")
    grad_rows = gather_rows(upstream_low, "a")
    raised = jnp.dot(mlp_rows, up_whole, preferred_element_type=floats) + up_bias_here
    activated = jax.nn.gelu(raised, approximate=True).astype(halves)
    mlp_sum = scatter_rows(
        jnp.einsum("tf,df->td", activated, down_whole, preferred_element_type=floats).astype(
            halves
        ),
        "a",
    )
    block_out = swap_places((hidden1 + mlp_sum + down_bias.astype(floats)).astype(halves))

    down_grad = owned_grad(
        jnp.einsum("td,tf->df", grad_rows, activated, preferred_element_type=floats)
    )
    act_grad = jnp.dot(grad_rows, down_whole, preferred_element_type=floats)
    gelu_back = jax.vjp(partial(jax.nn.gelu, approximate=True), raised)[1]
    raised_grad = gelu_back(act_grad)[0].astype(halves)
    up_bias_part = jnp.sum(raised_grad, axis=0, dtype=floats)
    normed2_grad = scatter_rows(
        jnp.einsum("tf,df->td", raised_grad, up_whole, preferred_element_type=floats).astype(
            halves
        ),
        "a",
    )
    up_grad = owned_grad(
        jnp.einsum("td,tf->df", mlp_rows, raised_grad, preferred_element_type=floats)
    )
    lower_second, gain2_grad, shift2_grad = normalize_back(
        normed2_grad, scaled2, inverse2, gain_second
    )
    hidden1_grad = upstream + lower_second
    attn_grad_rows = gather_rows(hidden1_grad.astype(halves), "a")
    up_spread = lax.dynamic_update_slice(
        jnp.zeros((FF,), floats), up_bias_part, (role * hidden,)
    )
    early = sum_everywhere(
        jnp.concatenate(
            [
                up_spread,
                jnp.sum(upstream, axis=0),
                jnp.sum(hidden1_grad, axis=0),
                gain2_grad,
                shift2_grad,
            ]
        ).reshape(-1, D)
    ).reshape(-1)
    mixed_grad = jnp.dot(attn_grad_rows, out_whole, preferred_element_type=floats).astype(halves)
    out_grad = owned_grad(
        jnp.einsum("td,tf->df", attn_grad_rows, mixed, preferred_element_type=floats)
    )
    query_grad, key_grad, value_grad, bias_parts = attention_backward(
        queries, keys_all, values_all, mixed_grad, lse, slopes, heads, seq_length
    )
    qkv_grad = jnp.concatenate([query_grad, key_grad, value_grad], axis=1)
    normed1_grad = scatter_rows(
        jnp.einsum("tf,df->td", qkv_grad, qkv_whole, preferred_element_type=floats).astype(
            halves
        ),
        "a",
    )
    qkv_weight_grad = owned_grad(
        jnp.einsum("td,tf->df", attn_rows, qkv_grad, preferred_element_type=floats)
    )
    lower_first, gain1_grad, shift1_grad = normalize_back(
        normed1_grad, scaled1, inverse1, gain_first
    )
    input_grad = swap_places((hidden1_grad + lower_first).astype(halves)).astype(floats)
    qv_spread = lax.dynamic_update_slice(
        jnp.zeros((2, D), floats), jnp.sum(bias_parts, axis=0), (0, role * width)
    )
    late = sum_everywhere(jnp.concatenate([qv_spread, gain1_grad[None], shift1_grad[None]]))
    return (
        block_out,
        input_grad,
        qkv_weight_grad.reshape(shard_rows, 3, width),
        lax.dynamic_slice_in_dim(late[:2], owner * width, width, 1),
        out_grad.T,
        early[FF + D : FF + 2 * D],
        up_grad,
        lax.dynamic_slice_in_dim(early[:FF], owner * hidden, hidden, 0),
        down_grad.T,
        early[FF : FF + D],
        late[2],
        late[3],
        early[FF + 2 * D : FF + 3 * D],
        early[FF + 3 * D :],
    )


def solution(mesh):
    rows, side = mesh.devices.shape
    names = ("y", "a", "z")
    split = Mesh(mesh.devices.reshape(rows // side, side, side), names)
    fsdp = ("y", "a")
    return jax.shard_map(
        body,
        mesh=split,
        in_specs=(
            P(names, None),
            P(fsdp, None, "z"),
            P(None, "z"),
            P("z", fsdp),
            P(),
            P(fsdp, "z"),
            P("z"),
            P("z", fsdp),
            P(),
            P(),
            P(),
            P(),
            P(),
            P(names, None),
        ),
        out_specs=(
            P(names, None),
            P(names, None),
            P(fsdp, None, "z"),
            P(None, "z"),
            P("z", fsdp),
            P(),
            P(fsdp, "z"),
            P("z"),
            P("z", fsdp),
            P(),
            P(),
            P(),
            P(),
            P(),
        ),
        check_vma=False,
    )
```

```python
from functools import partial

import jax
import jax.numpy as jnp
from jax import lax
from jax.experimental import pallas as pl
from jax.experimental.pallas import tpu as pltpu
from jax.sharding import Mesh, PartitionSpec as P

D = 1024
HEADS = 16
HEAD_DIM = 64
FF = 4096
SEQ_LEN = 1024


layer_eps = 1e-05


def normalize(rows, norm_gain, norm_shift):
    average = jnp.mean(rows, axis=1, keepdims=True)
    centred = rows - average
    spread = jnp.mean(centred * centred, axis=1, keepdims=True)
    inverse = lax.rsqrt(spread + layer_eps)
    scaled = centred * inverse
    return (scaled * norm_gain + norm_shift, scaled, inverse)


def normalize_back(upper, scaled, inverse, norm_gain):
    gain_grad = jnp.sum(upper * scaled, axis=0)
    shift_grad = jnp.sum(upper, axis=0)
    inner = upper * norm_gain
    lower = inverse * (
        inner
        - jnp.mean(inner, axis=1, keepdims=True)
        - scaled * jnp.mean(inner * scaled, axis=1, keepdims=True)
    )
    return (lower, gain_grad, shift_grad)


def head_mask(shape, head):
    lanes = lax.broadcasted_iota(jnp.int32, shape, 1)
    return (lanes >= head * HEAD_DIM) & (lanes < (head + 1) * HEAD_DIM)


def rows_dot(left, right):
    return lax.dot_general(
        left, right, (((1,), (1,)), ((), ())), preferred_element_type=jnp.float32
    )


def cols_dot(left, right):
    return lax.dot_general(
        left, right, (((0,), (0,)), ((), ())), preferred_element_type=jnp.float32
    )


def block_scores(query_block, keys_seen, slope, start, finish):
    raw = rows_dot(query_block, keys_seen) * HEAD_DIM ** (-0.5)
    shape = raw.shape
    offsets = lax.broadcasted_iota(jnp.int32, shape, 1) - (
        lax.broadcasted_iota(jnp.int32, shape, 0) + start
    )
    scores = raw + slope * offsets.astype(jnp.float32)
    return jnp.where(offsets <= 0, scores, -1e30)


def forward_kernel(heads, block_rows, slopes_ref, q_ref, k_ref, v_ref, mixed_ref, lse_ref):
    length, width = q_ref.shape
    for start in range(0, length, block_rows):
        finish = start + block_rows
        query_block = q_ref[start:finish]
        keys_seen = k_ref[:finish]
        values_seen = v_ref[:finish]
        out = jnp.zeros((block_rows, width), jnp.float32)
        lse = jnp.zeros((block_rows, 128), jnp.float32)
        lanes = lax.broadcasted_iota(jnp.int32, lse.shape, 1)
        zero = jnp.zeros_like(query_block)
        for head in range(heads):
            mask = head_mask(query_block.shape, head)
            scores = block_scores(
                jnp.where(mask, query_block, zero), keys_seen, slopes_ref[head], start, finish
            )
            top = jnp.max(scores, axis=1, keepdims=True)
            terms = jnp.exp(scores - top)
            total = jnp.sum(terms, axis=1, keepdims=True)
            probability = (terms * (1.0 / total)).astype(jnp.bfloat16)
            part = jnp.dot(probability, values_seen, preferred_element_type=jnp.float32)
            out = jnp.where(head_mask(out.shape, head), part, out)
            lse = jnp.where(lanes == head, top + jnp.log(total), lse)
        mixed_ref[start:finish] = out.astype(jnp.bfloat16)
        lse_ref[start:finish] = lse


def backward_kernel(
    heads,
    block_rows,
    slopes_ref,
    q_ref,
    k_ref,
    v_ref,
    grad_ref,
    lse_ref,
    dq_ref,
    dk_ref,
    dv_ref,
    bias_ref,
    dk_total,
    dv_total,
):
    length, width = q_ref.shape
    dk_total[...] = jnp.zeros_like(dk_total)
    dv_total[...] = jnp.zeros_like(dv_total)
    dq_sum = jnp.zeros((1, width), jnp.float32)
    for start in range(0, length, block_rows):
        finish = start + block_rows
        query_block = q_ref[start:finish]
        grad_block = grad_ref[start:finish]
        keys_seen = k_ref[:finish]
        values_seen = v_ref[:finish]
        zero = jnp.zeros_like(query_block)
        dq = jnp.zeros((block_rows, width), jnp.float32)
        for head in range(heads):
            mask = head_mask(query_block.shape, head)
            query_head = jnp.where(mask, query_block, zero)
            grad_head = jnp.where(mask, grad_block, zero)
            scores = block_scores(query_head, keys_seen, slopes_ref[head], start, finish)
            probability = jnp.exp(scores - lse_ref[start:finish, head : head + 1])
            prob_grad = rows_dot(grad_head, values_seen)
            centre = jnp.sum(probability * prob_grad, axis=1, keepdims=True)
            score_grad = (probability * (prob_grad - centre) * HEAD_DIM ** (-0.5)).astype(
                jnp.bfloat16
            )
            part = jnp.dot(score_grad, keys_seen, preferred_element_type=jnp.float32)
            dq = jnp.where(head_mask(dq.shape, head), part, dq)
            dk_total[:finish] += cols_dot(score_grad, query_head)
            dv_total[:finish] += cols_dot(probability.astype(jnp.bfloat16), grad_head)
        dq_low = dq.astype(jnp.bfloat16)
        dq_ref[start:finish] = dq_low
        dq_sum += jnp.sum(dq_low.astype(jnp.float32), axis=0, keepdims=True)
    dk_ref[...] = dk_total[...].astype(jnp.bfloat16)
    dv_low = dv_total[...].astype(jnp.bfloat16)
    dv_ref[...] = dv_low
    dv_sum = jnp.sum(dv_low.astype(jnp.float32), axis=0, keepdims=True)
    bias_ref[0, 0:1] = dq_sum
    bias_ref[0, 1:2] = dv_sum


def attention_forward(queries, keys_all, values_all, slopes, heads, seq_length):
    rows, width = queries.shape
    block = pl.BlockSpec((seq_length, width), lambda s: (s, 0))
    return pl.pallas_call(
        partial(forward_kernel, heads, min(256, seq_length)),
        grid=(rows // seq_length,),
        in_specs=[pl.BlockSpec(memory_space=pltpu.SMEM), block, block, block],
        out_specs=[block, pl.BlockSpec((seq_length, 128), lambda s: (s, 0))],
        out_shape=[
            jax.ShapeDtypeStruct((rows, width), jnp.bfloat16),
            jax.ShapeDtypeStruct((rows, 128), jnp.float32),
        ],
        compiler_params=pltpu.CompilerParams(vmem_limit_bytes=40 * 2**20),
        cost_estimate=pl.CostEstimate(
            flops=4 * heads * rows * seq_length * HEAD_DIM,
            bytes_accessed=10 * rows * width,
            transcendentals=heads * rows * seq_length // 2,
        ),
        name="attention_forward",
    )(slopes, queries, keys_all, values_all)


def attention_backward(queries, keys_all, values_all, mixed_grad, lse, slopes, heads, seq_length):
    rows, width = queries.shape
    seqs = rows // seq_length
    block = pl.BlockSpec((seq_length, width), lambda s: (s, 0))
    low = jax.ShapeDtypeStruct((rows, width), jnp.bfloat16)
    return pl.pallas_call(
        partial(backward_kernel, heads, min(256, seq_length)),
        grid=(seqs,),
        in_specs=[pl.BlockSpec(memory_space=pltpu.SMEM)]
        + [block] * 4
        + [pl.BlockSpec((seq_length, 128), lambda s: (s, 0))],
        out_specs=[block, block, block, pl.BlockSpec((1, 2, width), lambda s: (s, 0, 0))],
        out_shape=[low, low, low, jax.ShapeDtypeStruct((seqs, 2, width), jnp.float32)],
        scratch_shapes=[pltpu.VMEM((seq_length, width), jnp.float32)] * 2,
        compiler_params=pltpu.CompilerParams(vmem_limit_bytes=40 * 2**20),
        cost_estimate=pl.CostEstimate(
            flops=10 * heads * rows * seq_length * HEAD_DIM,
            bytes_accessed=14 * rows * width,
            transcendentals=heads * rows * seq_length // 2,
        ),
        name="attention_backward",
    )(slopes, queries, keys_all, values_all, mixed_grad, lse)


def swap_places(array):
    lines, side = lax.axis_size("y"), lax.axis_size("a")
    pairs = [
        ((y * side + a) * side + z, (y * side + z) * side + a)
        for y in range(lines)
        for a in range(side)
        for z in range(side)
    ]
    return lax.ppermute(array, ("y", "a", "z"), pairs)


def exchange(array, axis, mask):
    size = lax.axis_size(axis)
    return lax.ppermute(array, axis, [(i, i ^ mask) for i in range(size)])


def masks_of(size):
    return [1 << bit for bit in reversed(range(size.bit_length() - 1))]


def gather_rows(block, axis):
    size = lax.axis_size(axis)
    index = lax.axis_index(axis)
    held = block
    for place, mask in enumerate(masks_of(size)):
        other = exchange(held, axis, mask)
        upper = (index & mask) != 0
        held = jnp.stack(
            [jnp.where(upper, other, held), jnp.where(upper, held, other)], axis=place
        )
    return held.reshape((size * block.shape[0],) + block.shape[1:])


def scatter_rows(array, axis):
    size = lax.axis_size(axis)
    index = lax.axis_index(axis)
    masks = masks_of(size)
    held = array.reshape((2,) * len(masks) + (array.shape[0] // size,) + array.shape[1:])
    for place, mask in reversed(list(enumerate(masks))):
        upper = (index & mask) != 0
        first = lax.index_in_dim(held, 0, place, keepdims=False)
        second = lax.index_in_dim(held, 1, place, keepdims=False)
        sent = jnp.where(upper, first, second).astype(jnp.bfloat16)
        kept = jnp.where(upper, second, first).astype(jnp.float32)
        held = kept + exchange(sent, axis, mask).astype(jnp.float32)
    return held.astype(jnp.float32)


def whole_weight(shard):
    return gather_rows(lax.all_gather(shard, "z", axis=0, tiled=True), "y")


def owned_grad(grad):
    half = scatter_rows(grad.astype(jnp.bfloat16), "y").astype(jnp.bfloat16)
    part = lax.psum_scatter(half, "z", scatter_dimension=0, tiled=True)
    return swap_places(part).astype(jnp.float32)


def partner_of(index, masks):
    for mask in masks:
        index = index + mask * (1 - 2 * (index // mask % 2))
    return index


def bits_of(subset):
    return [1 << bit for bit in range(subset.bit_length()) if subset >> bit & 1]


def greet(devices):
    barrier = pltpu.get_barrier_semaphore()
    for device in devices:
        pl.semaphore_signal(
            barrier, inc=1, device_id=device, device_id_type=pl.DeviceIdType.MESH
        )
    pl.semaphore_wait(barrier, len(devices))


def gather_kernel(size, block_ref, whole_ref, send_sem, recv_sem):
    me = lax.axis_index("a")
    masks = masks_of(size)
    greet([{"a": partner_of(me, [mask])} for mask in masks])

    def copy_of(mask, subset):
        block = whole_ref.at[partner_of(me, bits_of(subset))]
        return pltpu.make_async_remote_copy(
            src_ref=block_ref if subset == 0 else block,
            dst_ref=block,
            send_sem=send_sem.at[slots[mask, subset]],
            recv_sem=recv_sem.at[slots[mask, subset]],
            device_id={"a": partner_of(me, [mask])},
            device_id_type=pl.DeviceIdType.MESH,
        )

    held = [0]
    slots = {}
    for mask in masks:
        for subset in held:
            slots[mask, subset] = len(slots)
        held = held + [subset | mask for subset in held]
    copies = {}
    for mask in masks:
        copies[mask, 0] = copy_of(mask, 0)
        copies[mask, 0].start()
    whole_ref[me] = block_ref[...]
    held = [0]
    for mask in masks:
        for subset in held:
            if subset:
                copies[mask, subset] = copy_of(mask, subset)
                copies[mask, subset].start()
        for subset in held:
            copies[mask, subset].wait_recv()
        held = held + [subset | mask for subset in held]
    for copy in copies.values():
        copy.wait_send()


def gather_side(block):
    size = lax.axis_size("a")
    whole = pl.pallas_call(
        partial(gather_kernel, size),
        out_shape=jax.ShapeDtypeStruct((size,) + block.shape, block.dtype),
        in_specs=[pl.BlockSpec(memory_space=pltpu.VMEM)],
        out_specs=pl.BlockSpec(memory_space=pltpu.VMEM),
        scratch_shapes=[pltpu.SemaphoreType.DMA((size - 1,))] * 2,
        compiler_params=pltpu.CompilerParams(
            collective_id=0, has_side_effects=True, vmem_limit_bytes=40 * 2**20
        ),
        name="gather_side",
    )(block)
    return whole.reshape((size * block.shape[0],) + block.shape[1:])


def scatter_kernel(size, parts_ref, sum_ref, landed, outgoing, send_sem, recv_sem):
    me = lax.axis_index("a")
    masks = masks_of(size)[::-1]
    greet([{"a": partner_of(me, [mask])} for mask in masks])
    slots = {}
    for mask in masks:
        for above in reversed(range(0, size, 2 * mask)):
            slots[mask, above] = len(slots)

    def copy_of(mask, above):
        slot = slots[mask, above]
        if mask == 1:
            source = parts_ref.at[partner_of(me, [1] + bits_of(above))]
        else:
            source = outgoing.at[slot]
        return pltpu.make_async_remote_copy(
            src_ref=source,
            dst_ref=landed.at[slot],
            send_sem=send_sem.at[slot],
            recv_sem=recv_sem.at[slot],
            device_id={"a": partner_of(me, [mask])},
            device_id_type=pl.DeviceIdType.MESH,
        )

    copies = {key: copy_of(*key) for key in slots}
    for (mask, above), copy in copies.items():
        if mask == 1:
            copy.start()
    for subset in reversed(range(0, size, 2)):
        reach = bits_of(subset)[0] if subset else size
        total = parts_ref[partner_of(me, bits_of(subset))].astype(jnp.float32)
        for mask in masks:
            if mask < reach:
                copies[mask, subset].wait_recv()
                total = total + landed[slots[mask, subset]].astype(jnp.float32)
        if subset:
            key = (reach, subset - reach)
            outgoing[slots[key]] = total.astype(jnp.bfloat16)
            copies[key].start()
        else:
            sum_ref[...] = total
    for copy in copies.values():
        copy.wait_send()


def scatter_side(array):
    size = lax.axis_size("a")
    rows, width = array.shape[0] // size, array.shape[1]
    slots = pltpu.VMEM((size - 1, rows, width), jnp.bfloat16)
    return pl.pallas_call(
        partial(scatter_kernel, size),
        out_shape=jax.ShapeDtypeStruct((rows, width), jnp.float32),
        in_specs=[pl.BlockSpec(memory_space=pltpu.VMEM)],
        out_specs=pl.BlockSpec(memory_space=pltpu.VMEM),
        scratch_shapes=[slots, slots] + [pltpu.SemaphoreType.DMA((size - 1,))] * 2,
        compiler_params=pltpu.CompilerParams(
            collective_id=1, has_side_effects=True, vmem_limit_bytes=40 * 2**20
        ),
        name="scatter_side",
    )(array.reshape(size, rows, width))


def sum_kernel(shape, own_ref, total_ref, landed, send_sem, recv_sem):
    lines, side = shape
    line, across, place = (lax.axis_index(name) for name in ("y", "a", "z"))
    partners = [(line, across, partner_of(place, [mask])) for mask in masks_of(side)]
    partners += [(line, partner_of(across, [mask]), place) for mask in masks_of(side)]
    partners += [(partner_of(line, [mask]), across, place) for mask in masks_of(lines)]
    greet(partners)
    total_ref[...] = own_ref[...]
    for step, partner in enumerate(partners):
        copy = pltpu.make_async_remote_copy(
            src_ref=total_ref,
            dst_ref=landed.at[step],
            send_sem=send_sem.at[step],
            recv_sem=recv_sem.at[step],
            device_id=partner,
            device_id_type=pl.DeviceIdType.MESH,
        )
        copy.start()
        copy.wait()
        total_ref[...] += landed[step]


def sum_everywhere(array):
    lines, side = lax.axis_size("y"), lax.axis_size("a")
    steps = len(masks_of(lines)) + 2 * len(masks_of(side))
    return pl.pallas_call(
        partial(sum_kernel, (lines, side)),
        out_shape=jax.ShapeDtypeStruct(array.shape, array.dtype),
        in_specs=[pl.BlockSpec(memory_space=pltpu.VMEM)],
        out_specs=pl.BlockSpec(memory_space=pltpu.VMEM),
        scratch_shapes=[pltpu.VMEM((steps,) + array.shape, array.dtype)]
        + [pltpu.SemaphoreType.DMA((steps,))] * 2,
        compiler_params=pltpu.CompilerParams(collective_id=2, has_side_effects=True),
        name="sum_everywhere",
    )(array)


def body(
    inputs,
    qkv_weight,
    qv_bias,
    out_weight,
    out_bias,
    up_weight,
    up_bias,
    down_weight,
    down_bias,
    norm1_gain,
    norm1_shift,
    norm2_gain,
    norm2_shift,
    cotangent,
):
    floats = jnp.float32
    halves = jnp.bfloat16
    role = lax.axis_index("a")
    owner = lax.axis_index("z")
    shard_rows = qkv_weight.shape[0]
    width = qkv_weight.shape[2]
    hidden = up_weight.shape[1]
    heads = width // HEAD_DIM

    here = swap_places(inputs)
    biases = jnp.concatenate([qv_bias.reshape(-1), up_bias]).reshape(-1, 3 * width)
    first_pack = swap_places(
        jnp.concatenate([qkv_weight.reshape(shard_rows, 3 * width), biases], axis=0)
    )
    biases = first_pack[shard_rows:].reshape(-1)
    qv_here = biases[: 2 * width].reshape(2, width).astype(floats)
    up_bias_here = biases[2 * width :].astype(floats)
    second_pack = swap_places(jnp.concatenate([up_weight, out_weight.T, down_weight.T], axis=1))
    up_out = lax.all_gather(second_pack[:, : hidden + width], "z", axis=0, tiled=True)
    down_shard, up_out = lax.optimization_barrier((second_pack[:, hidden + width :], up_out))
    up_out = gather_rows(up_out, "y")
    up_whole, out_whole = up_out[:, :hidden], up_out[:, hidden:]
    down_whole = whole_weight(down_shard)
    qkv_whole = whole_weight(first_pack[:shard_rows])
    upstream_low = swap_places(cotangent)
    upstream = upstream_low.astype(floats)

    input_float = here.astype(floats)
    gain_first = norm1_gain.astype(floats)
    gain_second = norm2_gain.astype(floats)
    normed1, scaled1, inverse1 = normalize(input_float, gain_first, norm1_shift.astype(floats))
    attn_rows = gather_side(normed1.astype(halves))
    seq_length = min(SEQ_LEN, attn_rows.shape[0])
    head_index = role * heads + jnp.arange(heads)
    slopes = jnp.exp2(-8.0 * (head_index.astype(floats) + 1.0) / HEADS)

    projected = jnp.dot(attn_rows, qkv_whole, preferred_element_type=floats)
    queries = (projected[:, :width] + qv_here[0]).astype(halves)
    keys_all = projected[:, width : 2 * width].astype(halves)
    values_all = (projected[:, 2 * width :] + qv_here[1]).astype(halves)
    mixed, lse = attention_forward(queries, keys_all, values_all, slopes, heads, seq_length)
    attn_sum = scatter_side(
        jnp.einsum("tf,df->td", mixed, out_whole, preferred_element_type=floats).astype(halves)
    )
    hidden1 = input_float + attn_sum + out_bias.astype(floats)
    normed2, scaled2, inverse2 = normalize(hidden1, gain_second, norm2_shift.astype(floats))
    mlp_rows = gather_side(normed2.astype(halves))
    grad_rows = gather_rows(upstream_low, "a")
    raised = jnp.dot(mlp_rows, up_whole, preferred_element_type=floats) + up_bias_here
    activated = jax.nn.gelu(raised, approximate=True).astype(halves)
    mlp_sum = scatter_rows(
        jnp.einsum("tf,df->td", activated, down_whole, preferred_element_type=floats).astype(
            halves
        ),
        "a",
    )
    block_out = swap_places((hidden1 + mlp_sum + down_bias.astype(floats)).astype(halves))

    down_grad = owned_grad(
        jnp.einsum("td,tf->df", grad_rows, activated, preferred_element_type=floats)
    )
    act_grad = jnp.dot(grad_rows, down_whole, preferred_element_type=floats)
    gelu_back = jax.vjp(partial(jax.nn.gelu, approximate=True), raised)[1]
    raised_grad = gelu_back(act_grad)[0].astype(halves)
    up_bias_part = jnp.sum(raised_grad, axis=0, dtype=floats)
    normed2_grad = scatter_side(
        jnp.einsum("tf,df->td", raised_grad, up_whole, preferred_element_type=floats).astype(
            halves
        )
    )
    up_grad = owned_grad(
        jnp.einsum("td,tf->df", mlp_rows, raised_grad, preferred_element_type=floats)
    )
    lower_second, gain2_grad, shift2_grad = normalize_back(
        normed2_grad, scaled2, inverse2, gain_second
    )
    hidden1_grad = upstream + lower_second
    attn_grad_rows = gather_side(hidden1_grad.astype(halves))
    mixed_grad = jnp.dot(attn_grad_rows, out_whole, preferred_element_type=floats).astype(halves)
    query_grad, key_grad, value_grad, bias_parts = attention_backward(
        queries, keys_all, values_all, mixed_grad, lse, slopes, heads, seq_length
    )
    qkv_grad = jnp.concatenate([query_grad, key_grad, value_grad], axis=1)
    normed1_grad = scatter_side(
        jnp.einsum("tf,df->td", qkv_grad, qkv_whole, preferred_element_type=floats).astype(
            halves
        )
    )
    joint_grad = owned_grad(
        jnp.concatenate(
            [
                jnp.einsum("td,tf->df", attn_rows, qkv_grad, preferred_element_type=floats),
                jnp.einsum("td,tf->df", attn_grad_rows, mixed, preferred_element_type=floats),
            ],
            axis=1,
        )
    )
    lower_first, gain1_grad, shift1_grad = normalize_back(
        normed1_grad, scaled1, inverse1, gain_first
    )
    input_grad = swap_places((hidden1_grad + lower_first).astype(halves)).astype(floats)
    up_spread = lax.dynamic_update_slice(
        jnp.zeros((FF,), floats), up_bias_part, (role * hidden,)
    )
    qv_spread = lax.dynamic_update_slice(
        jnp.zeros((2, D), floats), jnp.sum(bias_parts, axis=0), (0, role * width)
    )
    column_sums = [
        jnp.sum(hidden1_grad, axis=0),
        jnp.sum(upstream, axis=0),
        gain1_grad,
        shift1_grad,
        gain2_grad,
        shift2_grad,
    ]
    sums = sum_everywhere(
        jnp.concatenate([up_spread.reshape(-1, D), qv_spread, jnp.stack(column_sums)])
    )
    ups = FF // D
    return (
        block_out,
        input_grad,
        joint_grad[:, : 3 * width].reshape(shard_rows, 3, width),
        lax.dynamic_slice_in_dim(sums[ups : ups + 2], owner * width, width, 1),
        joint_grad[:, 3 * width :].T,
        sums[ups + 2],
        up_grad,
        lax.dynamic_slice_in_dim(sums[:ups].reshape(-1), owner * hidden, hidden, 0),
        down_grad.T,
        sums[ups + 3],
        sums[ups + 4],
        sums[ups + 5],
        sums[ups + 6],
        sums[ups + 7],
    )


def solution(mesh):
    rows, side = mesh.devices.shape
    names = ("y", "a", "z")
    split = Mesh(mesh.devices.reshape(rows // side, side, side), names)
    fsdp = ("y", "a")
    return jax.shard_map(
        body,
        mesh=split,
        in_specs=(
            P(names, None),
            P(fsdp, None, "z"),
            P(None, "z"),
            P("z", fsdp),
            P(),
            P(fsdp, "z"),
            P("z"),
            P("z", fsdp),
            P(),
            P(),
            P(),
            P(),
            P(),
            P(names, None),
        ),
        out_specs=(
            P(names, None),
            P(names, None),
            P(fsdp, None, "z"),
            P(None, "z"),
            P("z", fsdp),
            P(),
            P(fsdp, "z"),
            P("z"),
            P("z", fsdp),
            P(),
            P(),
            P(),
            P(),
            P(),
        ),
        check_vma=False,
    )
```

```python
from functools import partial

import jax
import jax.numpy as jnp
from jax import lax
from jax.experimental import pallas as pl
from jax.experimental.layout import Layout, with_layout_constraint
from jax.experimental.pallas import tpu as pltpu
from jax.sharding import Mesh, PartitionSpec as P

D = 1024
HEADS = 16
HEAD_DIM = 64
FF = 4096
SEQ_LEN = 1024


layer_eps = 1e-05


def normalize(rows, norm_gain, norm_shift):
    average = jnp.mean(rows, axis=1, keepdims=True)
    centred = rows - average
    spread = jnp.mean(centred * centred, axis=1, keepdims=True)
    inverse = lax.rsqrt(spread + layer_eps)
    scaled = centred * inverse
    return (scaled * norm_gain + norm_shift, scaled, inverse)


def normalize_back(upper, scaled, inverse, norm_gain):
    gain_grad = jnp.sum(upper * scaled, axis=0)
    shift_grad = jnp.sum(upper, axis=0)
    inner = upper * norm_gain
    lower = inverse * (
        inner
        - jnp.mean(inner, axis=1, keepdims=True)
        - scaled * jnp.mean(inner * scaled, axis=1, keepdims=True)
    )
    return (lower, gain_grad, shift_grad)


def head_mask(shape, head):
    lanes = lax.broadcasted_iota(jnp.int32, shape, 1)
    return (lanes >= head * HEAD_DIM) & (lanes < (head + 1) * HEAD_DIM)


def rows_dot(left, right):
    return lax.dot_general(
        left, right, (((1,), (1,)), ((), ())), preferred_element_type=jnp.float32
    )


def cols_dot(left, right):
    return lax.dot_general(
        left, right, (((0,), (0,)), ((), ())), preferred_element_type=jnp.float32
    )


def block_scores(query_block, keys_seen, slope, start, finish):
    raw = rows_dot(query_block, keys_seen) * HEAD_DIM ** (-0.5)
    shape = raw.shape
    offsets = lax.broadcasted_iota(jnp.int32, shape, 1) - (
        lax.broadcasted_iota(jnp.int32, shape, 0) + start
    )
    scores = raw + slope * offsets.astype(jnp.float32)
    return jnp.where(offsets <= 0, scores, -1e30)


def forward_kernel(heads, block_rows, slopes_ref, q_ref, k_ref, v_ref, mixed_ref, lse_ref):
    length, width = q_ref.shape
    for start in range(0, length, block_rows):
        finish = start + block_rows
        query_block = q_ref[start:finish]
        keys_seen = k_ref[:finish]
        values_seen = v_ref[:finish]
        out = jnp.zeros((block_rows, width), jnp.float32)
        lse = jnp.zeros((block_rows, 128), jnp.float32)
        lanes = lax.broadcasted_iota(jnp.int32, lse.shape, 1)
        zero = jnp.zeros_like(query_block)
        for head in range(heads):
            mask = head_mask(query_block.shape, head)
            scores = block_scores(
                jnp.where(mask, query_block, zero), keys_seen, slopes_ref[head], start, finish
            )
            top = jnp.max(scores, axis=1, keepdims=True)
            terms = jnp.exp(scores - top)
            total = jnp.sum(terms, axis=1, keepdims=True)
            probability = (terms * (1.0 / total)).astype(jnp.bfloat16)
            part = jnp.dot(probability, values_seen, preferred_element_type=jnp.float32)
            out = jnp.where(head_mask(out.shape, head), part, out)
            lse = jnp.where(lanes == head, top + jnp.log(total), lse)
        mixed_ref[start:finish] = out.astype(jnp.bfloat16)
        lse_ref[start:finish] = lse


def backward_kernel(
    heads,
    block_rows,
    slopes_ref,
    q_ref,
    k_ref,
    v_ref,
    grad_ref,
    lse_ref,
    dq_ref,
    dk_ref,
    dv_ref,
    bias_ref,
    dk_total,
    dv_total,
):
    length, width = q_ref.shape
    dk_total[...] = jnp.zeros_like(dk_total)
    dv_total[...] = jnp.zeros_like(dv_total)
    dq_sum = jnp.zeros((1, width), jnp.float32)
    for start in range(0, length, block_rows):
        finish = start + block_rows
        query_block = q_ref[start:finish]
        grad_block = grad_ref[start:finish]
        keys_seen = k_ref[:finish]
        values_seen = v_ref[:finish]
        zero = jnp.zeros_like(query_block)
        dq = jnp.zeros((block_rows, width), jnp.float32)
        for head in range(heads):
            mask = head_mask(query_block.shape, head)
            query_head = jnp.where(mask, query_block, zero)
            grad_head = jnp.where(mask, grad_block, zero)
            scores = block_scores(query_head, keys_seen, slopes_ref[head], start, finish)
            probability = jnp.exp(scores - lse_ref[start:finish, head : head + 1])
            prob_grad = rows_dot(grad_head, values_seen)
            centre = jnp.sum(probability * prob_grad, axis=1, keepdims=True)
            score_grad = (probability * (prob_grad - centre) * HEAD_DIM ** (-0.5)).astype(
                jnp.bfloat16
            )
            part = jnp.dot(score_grad, keys_seen, preferred_element_type=jnp.float32)
            dq = jnp.where(head_mask(dq.shape, head), part, dq)
            dk_total[:finish] += cols_dot(score_grad, query_head)
            dv_total[:finish] += cols_dot(probability.astype(jnp.bfloat16), grad_head)
        dq_low = dq.astype(jnp.bfloat16)
        dq_ref[start:finish] = dq_low
        dq_sum += jnp.sum(dq_low.astype(jnp.float32), axis=0, keepdims=True)
    dk_ref[...] = dk_total[...].astype(jnp.bfloat16)
    dv_low = dv_total[...].astype(jnp.bfloat16)
    dv_ref[...] = dv_low
    dv_sum = jnp.sum(dv_low.astype(jnp.float32), axis=0, keepdims=True)
    bias_ref[0, 0:1] = dq_sum
    bias_ref[0, 1:2] = dv_sum


def attention_forward(queries, keys_all, values_all, slopes, heads, seq_length):
    rows, width = queries.shape
    block = pl.BlockSpec((seq_length, width), lambda s: (s, 0))
    return pl.pallas_call(
        partial(forward_kernel, heads, min(256, seq_length)),
        grid=(rows // seq_length,),
        in_specs=[pl.BlockSpec(memory_space=pltpu.SMEM), block, block, block],
        out_specs=[block, pl.BlockSpec((seq_length, 128), lambda s: (s, 0))],
        out_shape=[
            jax.ShapeDtypeStruct((rows, width), jnp.bfloat16),
            jax.ShapeDtypeStruct((rows, 128), jnp.float32),
        ],
        compiler_params=pltpu.CompilerParams(vmem_limit_bytes=40 * 2**20),
        cost_estimate=pl.CostEstimate(
            flops=4 * heads * rows * seq_length * HEAD_DIM,
            bytes_accessed=10 * rows * width,
            transcendentals=heads * rows * seq_length // 2,
        ),
        name="attention_forward",
    )(slopes, queries, keys_all, values_all)


def attention_backward(queries, keys_all, values_all, mixed_grad, lse, slopes, heads, seq_length):
    rows, width = queries.shape
    seqs = rows // seq_length
    block = pl.BlockSpec((seq_length, width), lambda s: (s, 0))
    low = jax.ShapeDtypeStruct((rows, width), jnp.bfloat16)
    return pl.pallas_call(
        partial(backward_kernel, heads, min(256, seq_length)),
        grid=(seqs,),
        in_specs=[pl.BlockSpec(memory_space=pltpu.SMEM)]
        + [block] * 4
        + [pl.BlockSpec((seq_length, 128), lambda s: (s, 0))],
        out_specs=[block, block, block, pl.BlockSpec((1, 2, width), lambda s: (s, 0, 0))],
        out_shape=[low, low, low, jax.ShapeDtypeStruct((seqs, 2, width), jnp.float32)],
        scratch_shapes=[pltpu.VMEM((seq_length, width), jnp.float32)] * 2,
        compiler_params=pltpu.CompilerParams(vmem_limit_bytes=40 * 2**20),
        cost_estimate=pl.CostEstimate(
            flops=10 * heads * rows * seq_length * HEAD_DIM,
            bytes_accessed=14 * rows * width,
            transcendentals=heads * rows * seq_length // 2,
        ),
        name="attention_backward",
    )(slopes, queries, keys_all, values_all, mixed_grad, lse)


def swap_places(array):
    lines, side = lax.axis_size("y"), lax.axis_size("a")
    pairs = [
        ((y * side + a) * side + z, (y * side + z) * side + a)
        for y in range(lines)
        for a in range(side)
        for z in range(side)
    ]
    return lax.ppermute(array, ("y", "a", "z"), pairs)


def exchange(array, axis, mask):
    size = lax.axis_size(axis)
    return lax.ppermute(array, axis, [(i, i ^ mask) for i in range(size)])


def masks_of(size):
    return [1 << bit for bit in reversed(range(size.bit_length() - 1))]


def gather_rows(block, axis):
    size = lax.axis_size(axis)
    index = lax.axis_index(axis)
    held = block
    for place, mask in enumerate(masks_of(size)):
        other = exchange(held, axis, mask)
        upper = (index & mask) != 0
        held = jnp.stack(
            [jnp.where(upper, other, held), jnp.where(upper, held, other)], axis=place
        )
    return held.reshape((size * block.shape[0],) + block.shape[1:])


def scatter_rows(array, axis):
    size = lax.axis_size(axis)
    index = lax.axis_index(axis)
    masks = masks_of(size)
    held = array.reshape((2,) * len(masks) + (array.shape[0] // size,) + array.shape[1:])
    for place, mask in reversed(list(enumerate(masks))):
        upper = (index & mask) != 0
        first = lax.index_in_dim(held, 0, place, keepdims=False)
        second = lax.index_in_dim(held, 1, place, keepdims=False)
        sent = jnp.where(upper, first, second).astype(jnp.bfloat16)
        kept = jnp.where(upper, second, first).astype(jnp.float32)
        held = kept + exchange(sent, axis, mask).astype(jnp.float32)
    return held.astype(jnp.float32)


def by_rows(array):
    return with_layout_constraint(array, Layout(major_to_minor=(0, 1)))


def whole_weight(shard):
    return by_rows(lax.all_gather(by_rows(shard), ("y", "z"), axis=0, tiled=True))


def owned_grad(grad):
    low = by_rows(grad.astype(jnp.bfloat16))
    part = lax.psum_scatter(low, ("y", "z"), scatter_dimension=0, tiled=True)
    return by_rows(swap_places(by_rows(part))).astype(jnp.float32)


def owned_grad_late(grad):
    half = by_rows(scatter_rows(by_rows(grad.astype(jnp.bfloat16)), "y").astype(jnp.bfloat16))
    part = lax.psum_scatter(half, "z", scatter_dimension=0, tiled=True)
    return by_rows(swap_places(by_rows(part))).astype(jnp.float32)


def partner_of(index, masks):
    for mask in masks:
        index = index + mask * (1 - 2 * (index // mask % 2))
    return index


def bits_of(subset):
    return [1 << bit for bit in range(subset.bit_length()) if subset >> bit & 1]


def greet(devices):
    barrier = pltpu.get_barrier_semaphore()
    for device in devices:
        pl.semaphore_signal(
            barrier, inc=1, device_id=device, device_id_type=pl.DeviceIdType.MESH
        )
    pl.semaphore_wait(barrier, len(devices))


def gather_kernel(size, block_ref, whole_ref, send_sem, recv_sem):
    me = lax.axis_index("a")
    masks = masks_of(size)
    greet([{"a": partner_of(me, [mask])} for mask in masks])

    def copy_of(mask, subset):
        block = whole_ref.at[partner_of(me, bits_of(subset))]
        return pltpu.make_async_remote_copy(
            src_ref=block_ref if subset == 0 else block,
            dst_ref=block,
            send_sem=send_sem.at[slots[mask, subset]],
            recv_sem=recv_sem.at[slots[mask, subset]],
            device_id={"a": partner_of(me, [mask])},
            device_id_type=pl.DeviceIdType.MESH,
        )

    held = [0]
    slots = {}
    for mask in masks:
        for subset in held:
            slots[mask, subset] = len(slots)
        held = held + [subset | mask for subset in held]
    copies = {}
    for mask in masks:
        copies[mask, 0] = copy_of(mask, 0)
        copies[mask, 0].start()
    whole_ref[me] = block_ref[...]
    held = [0]
    for mask in masks:
        for subset in held:
            if subset:
                copies[mask, subset] = copy_of(mask, subset)
                copies[mask, subset].start()
        for subset in held:
            copies[mask, subset].wait_recv()
        held = held + [subset | mask for subset in held]
    for copy in copies.values():
        copy.wait_send()


def gather_side(block):
    size = lax.axis_size("a")
    whole = pl.pallas_call(
        partial(gather_kernel, size),
        out_shape=jax.ShapeDtypeStruct((size,) + block.shape, block.dtype),
        in_specs=[pl.BlockSpec(memory_space=pltpu.VMEM)],
        out_specs=pl.BlockSpec(memory_space=pltpu.VMEM),
        scratch_shapes=[pltpu.SemaphoreType.DMA((size - 1,))] * 2,
        compiler_params=pltpu.CompilerParams(
            collective_id=0, has_side_effects=True, vmem_limit_bytes=40 * 2**20
        ),
        name="gather_side",
    )(block)
    return whole.reshape((size * block.shape[0],) + block.shape[1:])


def scatter_kernel(size, parts_ref, sum_ref, landed, outgoing, send_sem, recv_sem):
    me = lax.axis_index("a")
    masks = masks_of(size)[::-1]
    greet([{"a": partner_of(me, [mask])} for mask in masks])
    slots = {}
    for mask in masks:
        for above in reversed(range(0, size, 2 * mask)):
            slots[mask, above] = len(slots)

    def copy_of(mask, above):
        slot = slots[mask, above]
        if mask == 1:
            source = parts_ref.at[partner_of(me, [1] + bits_of(above))]
        else:
            source = outgoing.at[slot]
        return pltpu.make_async_remote_copy(
            src_ref=source,
            dst_ref=landed.at[slot],
            send_sem=send_sem.at[slot],
            recv_sem=recv_sem.at[slot],
            device_id={"a": partner_of(me, [mask])},
            device_id_type=pl.DeviceIdType.MESH,
        )

    copies = {key: copy_of(*key) for key in slots}
    for (mask, above), copy in copies.items():
        if mask == 1:
            copy.start()
    for subset in reversed(range(0, size, 2)):
        reach = bits_of(subset)[0] if subset else size
        total = parts_ref[partner_of(me, bits_of(subset))].astype(jnp.float32)
        for mask in masks:
            if mask < reach:
                copies[mask, subset].wait_recv()
                total = total + landed[slots[mask, subset]].astype(jnp.float32)
        if subset:
            key = (reach, subset - reach)
            outgoing[slots[key]] = total.astype(jnp.bfloat16)
            copies[key].start()
        else:
            sum_ref[...] = total
    for copy in copies.values():
        copy.wait_send()


def scatter_side(array):
    size = lax.axis_size("a")
    rows, width = array.shape[0] // size, array.shape[1]
    slots = pltpu.VMEM((size - 1, rows, width), jnp.bfloat16)
    return pl.pallas_call(
        partial(scatter_kernel, size),
        out_shape=jax.ShapeDtypeStruct((rows, width), jnp.float32),
        in_specs=[pl.BlockSpec(memory_space=pltpu.VMEM)],
        out_specs=pl.BlockSpec(memory_space=pltpu.VMEM),
        scratch_shapes=[slots, slots] + [pltpu.SemaphoreType.DMA((size - 1,))] * 2,
        compiler_params=pltpu.CompilerParams(
            collective_id=1, has_side_effects=True, vmem_limit_bytes=40 * 2**20
        ),
        name="scatter_side",
    )(array.reshape(size, rows, width))


def sum_kernel(shape, own_ref, total_ref, landed, send_sem, recv_sem):
    lines, side = shape
    line, across, place = (lax.axis_index(name) for name in ("y", "a", "z"))
    partners = [(line, across, partner_of(place, [mask])) for mask in masks_of(side)]
    partners += [(line, partner_of(across, [mask]), place) for mask in masks_of(side)]
    partners += [(partner_of(line, [mask]), across, place) for mask in masks_of(lines)]
    greet(partners)
    total_ref[...] = own_ref[...]
    for step, partner in enumerate(partners):
        copy = pltpu.make_async_remote_copy(
            src_ref=total_ref,
            dst_ref=landed.at[step],
            send_sem=send_sem.at[step],
            recv_sem=recv_sem.at[step],
            device_id=partner,
            device_id_type=pl.DeviceIdType.MESH,
        )
        copy.start()
        copy.wait()
        total_ref[...] += landed[step]


def sum_everywhere(array):
    lines, side = lax.axis_size("y"), lax.axis_size("a")
    steps = len(masks_of(lines)) + 2 * len(masks_of(side))
    return pl.pallas_call(
        partial(sum_kernel, (lines, side)),
        out_shape=jax.ShapeDtypeStruct(array.shape, array.dtype),
        in_specs=[pl.BlockSpec(memory_space=pltpu.VMEM)],
        out_specs=pl.BlockSpec(memory_space=pltpu.VMEM),
        scratch_shapes=[pltpu.VMEM((steps,) + array.shape, array.dtype)]
        + [pltpu.SemaphoreType.DMA((steps,))] * 2,
        compiler_params=pltpu.CompilerParams(collective_id=2, has_side_effects=True),
        name="sum_everywhere",
    )(array)


def body(
    inputs,
    qkv_weight,
    qv_bias,
    out_weight,
    out_bias,
    up_weight,
    up_bias,
    down_weight,
    down_bias,
    norm1_gain,
    norm1_shift,
    norm2_gain,
    norm2_shift,
    cotangent,
):
    floats = jnp.float32
    halves = jnp.bfloat16
    role = lax.axis_index("a")
    owner = lax.axis_index("z")
    shard_rows = qkv_weight.shape[0]
    width = qkv_weight.shape[2]
    hidden = up_weight.shape[1]
    heads = width // HEAD_DIM

    here = swap_places(inputs)
    biases = jnp.concatenate([qv_bias.reshape(-1), up_bias]).reshape(-1, 3 * width)
    first_pack = by_rows(
        swap_places(
            by_rows(
                jnp.concatenate([qkv_weight.reshape(shard_rows, 3 * width), biases], axis=0)
            )
        )
    )
    biases = first_pack[shard_rows:].reshape(-1)
    qv_here = biases[: 2 * width].reshape(2, width).astype(floats)
    up_bias_here = biases[2 * width :].astype(floats)
    qkv_shard = by_rows(first_pack[:shard_rows])
    qkv_whole = by_rows(
        gather_rows(by_rows(lax.all_gather(qkv_shard, "z", axis=0, tiled=True)), "y")
    )
    out_shard = swap_places(by_rows(out_weight.T))
    up_shard = swap_places(up_weight)
    down_shard = swap_places(by_rows(down_weight.T))
    out_whole = whole_weight(out_shard)
    up_shard, out_whole = lax.optimization_barrier((up_shard, out_whole))
    up_whole = whole_weight(up_shard)
    down_shard, up_whole = lax.optimization_barrier((down_shard, up_whole))
    down_whole = whole_weight(down_shard)
    upstream_low = swap_places(cotangent)
    upstream = upstream_low.astype(floats)

    input_float = here.astype(floats)
    gain_first = norm1_gain.astype(floats)
    gain_second = norm2_gain.astype(floats)
    normed1, scaled1, inverse1 = normalize(input_float, gain_first, norm1_shift.astype(floats))
    attn_rows = gather_side(normed1.astype(halves))
    seq_length = min(SEQ_LEN, attn_rows.shape[0])
    head_index = role * heads + jnp.arange(heads)
    slopes = jnp.exp2(-8.0 * (head_index.astype(floats) + 1.0) / HEADS)

    projected = jnp.dot(attn_rows, qkv_whole, preferred_element_type=floats)
    queries = (projected[:, :width] + qv_here[0]).astype(halves)
    keys_all = projected[:, width : 2 * width].astype(halves)
    values_all = (projected[:, 2 * width :] + qv_here[1]).astype(halves)
    mixed, lse = attention_forward(queries, keys_all, values_all, slopes, heads, seq_length)
    attn_sum = scatter_side(
        jnp.einsum("tf,df->td", mixed, out_whole, preferred_element_type=floats).astype(halves)
    )
    hidden1 = input_float + attn_sum + out_bias.astype(floats)
    normed2, scaled2, inverse2 = normalize(hidden1, gain_second, norm2_shift.astype(floats))
    mlp_rows = gather_side(normed2.astype(halves))
    grad_rows = gather_rows(upstream_low, "a")
    raised = jnp.dot(mlp_rows, up_whole, preferred_element_type=floats) + up_bias_here
    activated = jax.nn.gelu(raised, approximate=True).astype(halves)
    mlp_sum = scatter_rows(
        jnp.einsum("tf,df->td", activated, down_whole, preferred_element_type=floats).astype(
            halves
        ),
        "a",
    )
    block_out = swap_places((hidden1 + mlp_sum + down_bias.astype(floats)).astype(halves))

    down_grad = owned_grad(
        jnp.einsum("td,tf->df", grad_rows, activated, preferred_element_type=floats)
    )
    act_grad = jnp.dot(grad_rows, down_whole, preferred_element_type=floats)
    gelu_back = jax.vjp(partial(jax.nn.gelu, approximate=True), raised)[1]
    raised_grad = gelu_back(act_grad)[0].astype(halves)
    up_bias_part = jnp.sum(raised_grad, axis=0, dtype=floats)
    normed2_grad = scatter_side(
        jnp.einsum("tf,df->td", raised_grad, up_whole, preferred_element_type=floats).astype(
            halves
        )
    )
    up_grad = owned_grad(
        jnp.einsum("td,tf->df", mlp_rows, raised_grad, preferred_element_type=floats)
    )
    lower_second, gain2_grad, shift2_grad = normalize_back(
        normed2_grad, scaled2, inverse2, gain_second
    )
    hidden1_grad = upstream + lower_second
    attn_grad_rows = gather_side(hidden1_grad.astype(halves))
    mixed_grad = jnp.dot(attn_grad_rows, out_whole, preferred_element_type=floats).astype(halves)
    query_grad, key_grad, value_grad, bias_parts = attention_backward(
        queries, keys_all, values_all, mixed_grad, lse, slopes, heads, seq_length
    )
    qkv_grad = jnp.concatenate([query_grad, key_grad, value_grad], axis=1)
    normed1_grad = scatter_side(
        jnp.einsum("tf,df->td", qkv_grad, qkv_whole, preferred_element_type=floats).astype(
            halves
        )
    )
    joint_grad = owned_grad_late(
        jnp.concatenate(
            [
                jnp.einsum("td,tf->df", attn_rows, qkv_grad, preferred_element_type=floats),
                jnp.einsum("td,tf->df", attn_grad_rows, mixed, preferred_element_type=floats),
            ],
            axis=1,
        )
    )
    lower_first, gain1_grad, shift1_grad = normalize_back(
        normed1_grad, scaled1, inverse1, gain_first
    )
    input_grad = swap_places((hidden1_grad + lower_first).astype(halves)).astype(floats)
    up_spread = lax.dynamic_update_slice(
        jnp.zeros((FF,), floats), up_bias_part, (role * hidden,)
    )
    qv_spread = lax.dynamic_update_slice(
        jnp.zeros((2, D), floats), jnp.sum(bias_parts, axis=0), (0, role * width)
    )
    column_sums = [
        jnp.sum(hidden1_grad, axis=0),
        jnp.sum(upstream, axis=0),
        gain1_grad,
        shift1_grad,
        gain2_grad,
        shift2_grad,
    ]
    sums = sum_everywhere(
        jnp.concatenate([up_spread.reshape(-1, D), qv_spread, jnp.stack(column_sums)])
    )
    ups = FF // D
    return (
        block_out,
        input_grad,
        joint_grad[:, : 3 * width].reshape(shard_rows, 3, width),
        lax.dynamic_slice_in_dim(sums[ups : ups + 2], owner * width, width, 1),
        joint_grad[:, 3 * width :].T,
        sums[ups + 2],
        up_grad,
        lax.dynamic_slice_in_dim(sums[:ups].reshape(-1), owner * hidden, hidden, 0),
        down_grad.T,
        sums[ups + 3],
        sums[ups + 4],
        sums[ups + 5],
        sums[ups + 6],
        sums[ups + 7],
    )


def solution(mesh):
    rows, side = mesh.devices.shape
    names = ("y", "a", "z")
    split = Mesh(mesh.devices.reshape(rows // side, side, side), names)
    fsdp = ("y", "a")
    return jax.shard_map(
        body,
        mesh=split,
        in_specs=(
            P(names, None),
            P(fsdp, None, "z"),
            P(None, "z"),
            P("z", fsdp),
            P(),
            P(fsdp, "z"),
            P("z"),
            P("z", fsdp),
            P(),
            P(),
            P(),
            P(),
            P(),
            P(names, None),
        ),
        out_specs=(
            P(names, None),
            P(names, None),
            P(fsdp, None, "z"),
            P(None, "z"),
            P("z", fsdp),
            P(),
            P(fsdp, "z"),
            P("z"),
            P("z", fsdp),
            P(),
            P(),
            P(),
            P(),
            P(),
        ),
        check_vma=False,
    )
```
